256 devices in a mesh: dp: 32 (over z, x), tensor: 8 (over y, core).
Axes of the slice: x: 4, y: 4, z: 8, core: 2. Of those that a mesh axis runs over, the one named last changes fastest.
Arguments:
- queries: bfloat16 [16384, 8192], P('dp', 'tensor'), may hold values from -16 to 16
- key_rows: bfloat16 [16384, 1024], P('dp', 'tensor'), may hold values from -16 to 16
- value_matrix: bfloat16 [16384, 1024], P('dp', 'tensor'), may hold values from -6 to 6
- out_grad: bfloat16 [16384, 8192], P('dp', 'tensor'), may hold values from -6 to 6
- inputs: bfloat16 [16384, 8192], P('dp', 'tensor'), may hold values from -0.08984375 to 0.08984375
- doc_ids: int32 [16384], replicated, may hold values from 0 to 127, never falling along the last dimension, each value on 1 to 256 neighbouring positions
Outputs:
- attention_out: bfloat16 [16384, 8192], P('dp', 'tensor')
- query_grad: bfloat16 [16384, 8192], P('dp', 'tensor')
- key_gradient: bfloat16 [16384, 1024], P('dp', 'tensor')
- value_gradient: bfloat16 [16384, 1024], P('dp', 'tensor')
- softmax_logsum: float32 [64, 16384], P('tensor', 'dp')
- projection_weight_gradient: float32 [8192, 2048], P(('tensor', 'dp'))
The draws below stay inside these ranges and needn't reach their ends.
Inputs may be any that keep to these rules, and one draw needn't show every extreme that they name: `doc_ids`: document numbers never fall along the rows; each document is 1 to 256 consecutive rows, and some document has exactly 256.
All inputs are finite; a program needn't handle non-finite values.
Results may differ from the reference program's by a relative error of at most 0.02.
Values may be sent and summed in bfloat16 or wider, within the bound.
No kernel may reach another device: no remote copies, remote signals or barrier semaphores. Data moves between devices by JAX's collectives and lax.ppermute only.
A program may use at most 64 MiB of HBM per device.

```python
import math
import jax
import jax.numpy as jnp
import numpy as np
from jax import lax

MODEL_WIDTH = 8192
QUERY_HEADS = 64
KEY_VALUE_HEADS = 8
HEAD_SIZE = 128
TOK_DEV = 512
DOCUMENT_TOKENS = 256
TOKEN_ROWS_ALL = 16384
DOCUMENTS = 128
N_DP = 32


def draw_queries(key, part):
    key = jax.random.fold_in(key, 3)
    return jnp.clip(jax.random.normal(key, (TOKEN_ROWS_ALL, QUERY_HEADS * HEAD_SIZE), jnp.float32), -6.0, 6.0).astype(jnp.bfloat16)


def draw_key_rows(key, part):
    key = jax.random.fold_in(key, 5)
    return jnp.clip(jax.random.normal(key, (TOKEN_ROWS_ALL, KEY_VALUE_HEADS * HEAD_SIZE), jnp.float32), -6.0, 6.0).astype(jnp.bfloat16)


def spiked(entries, key, source, target, blocks, factor):
    def block_of(axis_at):
        return (jnp.arange(entries.shape[axis_at]) // (entries.shape[axis_at] // blocks)).reshape((-1,) + (1,) * (entries.ndim - 1 - axis_at))

    near = jax.random.permutation(key, blocks)[block_of(target)]
    second = (block_of(target) + blocks // 2) % blocks
    return jnp.where((block_of(source) == near) | (block_of(source) == second), factor * entries, entries)


def level_of(stream_key, dims, split, least, high):
    level, own = 1.0, jax.random.fold_in(stream_key, 6)
    for axis_at, blocks in split:
        draws = jnp.exp(jax.random.uniform(jax.random.fold_in(own, axis_at), (blocks,), jnp.float32, least / len(split), high / len(split)))
        level = level * jnp.repeat(draws, dims[axis_at] // blocks).reshape([-1 if axis == axis_at else 1 for axis in range(len(dims))])
    return level


def split_up(number_of, total, limit, slope):
    loads = [(1 << 20) // math.isqrt(grade ** slope) + 1 for grade in range(2, number_of + 1)]
    surplus, counts = total - limit - (number_of - 1), [1] * (number_of - 1)
    while surplus > 0:
        movable = [i for i in range(number_of - 1) if counts[i] < limit]
        mass, left = sum([loads[i] for i in movable]), surplus
        for i in movable:
            extra = min(limit - counts[i], max(1, left * loads[i] // mass), surplus)
            counts[i] = counts[i] + extra
            surplus = surplus - extra
    return np.array([limit] + counts)


def uneven(own_key, number_of, total, most, skew):
    if number_of == 2:
        one = jax.random.randint(own_key, (), max(1, total - most), min(most, total - 1) + 1)
        return jnp.stack([one, total - one])
    tallies = jnp.asarray(split_up(number_of, total, most, skew), jnp.int32)
    twos = (number_of - 1) // 2
    source_of, sink = tallies[1:1 + 2 * twos:2], tallies[2:2 + 2 * twos:2]
    slack = jnp.minimum(source_of - 1, most - sink)
    shifted = jax.random.randint(jax.random.fold_in(own_key, 1), (twos,), 0, 1 << 20) % (slack + 1)
    tallies = tallies.at[1:1 + 2 * twos:2].set(source_of - shifted).at[2:2 + 2 * twos:2].set(sink + shifted)
    return tallies[jax.random.permutation(jax.random.fold_in(own_key, 2), number_of)]


def normal_values(rng, extent, width, most, split=(), kind=jnp.bfloat16):
    result = width * jax.random.normal(rng, extent, jnp.float32)
    if split:
        result = result * level_of(rng, extent, split, -0.22, 0.18)
    return jnp.clip(result, -most, most).astype(kind)


def noise_with(own_key, extent, width, bound, pieces, heavy, kind=jnp.bfloat16):
    drawn = width * jax.random.normal(own_key, extent, jnp.float32)
    if pieces:
        drawn = drawn * level_of(own_key, extent, pieces, -0.22, 0.18)
    return jnp.clip(spiked(drawn, jax.random.fold_in(own_key, 3), *heavy), -bound, bound).astype(kind)


def setup_inputs(seed: int = 0) -> dict:
    streams_of = jax.random.split(jax.random.key(seed), 7)
    return {
        "queries": draw_queries(jax.random.fold_in(streams_of[6], 71), 0),
        "key_rows": draw_key_rows(jax.random.fold_in(streams_of[6], 71), 0),
        "value_matrix": normal_values(streams_of[2], (TOKEN_ROWS_ALL, KEY_VALUE_HEADS * HEAD_SIZE), 1.0, 6.0, ((0, 32), (1, 8))),
        "out_grad": normal_values(streams_of[3], (TOKEN_ROWS_ALL, QUERY_HEADS * HEAD_SIZE), 1.0, 6.0, ((0, 32), (1, 8))),
        "inputs": noise_with(streams_of[4], (TOKEN_ROWS_ALL, MODEL_WIDTH), 0.015, 0.08984375, ((0, 32), (1, 8)), (0, 1, 32, 2.75)),
        "doc_ids": jnp.searchsorted(jnp.cumsum(uneven(streams_of[5], DOCUMENTS, TOKEN_ROWS_ALL, DOCUMENT_TOKENS, 1)), jnp.arange(TOKEN_ROWS_ALL), side="right").astype(jnp.int32),
    }


def attend(query_rows, key_block, val_block, grad_rows, query_seg, key_seg, query_pos, key_pos):
    score_scale = query_rows.shape[-1] ** -0.5
    high = lax.Precision.HIGHEST
    query_f = query_rows.astype(jnp.float32)
    key_f = key_block.astype(jnp.float32)
    val_f = val_block.astype(jnp.float32)
    grad_f = grad_rows.astype(jnp.float32)
    scores = jnp.einsum("rgd,cd->grc", query_f, key_f, precision=high) * score_scale
    allowed = (query_seg[:, None] == key_seg[None, :]) & (key_pos[None, :] <= query_pos[:, None])
    masked = jnp.where(allowed[None], scores, -jnp.inf)
    row_max = jnp.max(masked, axis=-1)
    expd = jnp.where(allowed[None], jnp.exp(masked - row_max[..., None]), 0.0)
    totals = jnp.sum(expd, axis=-1)
    probs = expd / totals[..., None]
    logsum = row_max + jnp.log(totals)
    probs_low = lax.optimization_barrier(probs.astype(jnp.bfloat16))
    out_rows = jnp.einsum("grc,cd->rgd", probs_low.astype(jnp.float32), val_f, precision=high).astype(jnp.bfloat16)
    out_rows = lax.optimization_barrier(out_rows)
    delta = jnp.sum(grad_f * out_rows.astype(jnp.float32), axis=-1)
    dprobs = jnp.einsum("rgd,cd->grc", grad_f, val_f, precision=high)
    dscores = (score_scale * probs * (dprobs - delta.T[..., None])).astype(jnp.bfloat16)
    dscores_f = lax.optimization_barrier(dscores).astype(jnp.float32)
    query_grad = jnp.einsum("grc,cd->rgd", dscores_f, key_f, precision=high).astype(jnp.bfloat16)
    key_part = jnp.einsum("grc,rgd->cd", dscores_f, query_f, precision=high)
    value_part = jnp.einsum("grc,rgd->cd", probs_low.astype(jnp.float32), grad_f, precision=high)
    return out_rows, query_grad, key_part, value_part, logsum


def reference(queries, key_rows, value_matrix, out_grad, inputs, doc_ids):
    group_width = QUERY_HEADS // KEY_VALUE_HEADS
    reach_rows = DOCUMENT_TOKENS
    window = TOK_DEV + reach_rows
    key_pad = jnp.concatenate([jnp.zeros((reach_rows, KEY_VALUE_HEADS * HEAD_SIZE), jnp.bfloat16), key_rows], axis=0)
    val_pad = jnp.concatenate([jnp.zeros((reach_rows, KEY_VALUE_HEADS * HEAD_SIZE), jnp.bfloat16), value_matrix], axis=0)
    seg_pad = jnp.concatenate([jnp.full((reach_rows,), -1, jnp.int32), doc_ids.astype(jnp.int32)], axis=0)
    pos_pad = jnp.arange(TOKEN_ROWS_ALL + reach_rows, dtype=jnp.int32) - reach_rows
    per_head = jax.vmap(attend, in_axes=(1, 1, 1, 1, None, None, None, None), out_axes=(1, 1, 1, 1, 0))

    def one_shard(shard_id):
        first = (shard_id * TOK_DEV).astype(jnp.int32)
        query_part = lax.dynamic_slice_in_dim(queries, first, TOK_DEV, 0).reshape(TOK_DEV, KEY_VALUE_HEADS, group_width, HEAD_SIZE)
        grad_part = lax.dynamic_slice_in_dim(out_grad, first, TOK_DEV, 0).reshape(TOK_DEV, KEY_VALUE_HEADS, group_width, HEAD_SIZE)
        key_part = lax.dynamic_slice_in_dim(key_pad, first, window, 0).reshape(window, KEY_VALUE_HEADS, HEAD_SIZE)
        val_part = lax.dynamic_slice_in_dim(val_pad, first, window, 0).reshape(window, KEY_VALUE_HEADS, HEAD_SIZE)
        query_seg = lax.dynamic_slice_in_dim(doc_ids.astype(jnp.int32), first, TOK_DEV, 0)
        key_seg = lax.dynamic_slice_in_dim(seg_pad, first, window, 0)
        query_pos = first + jnp.arange(TOK_DEV, dtype=jnp.int32)
        key_pos = lax.dynamic_slice_in_dim(pos_pad, first, window, 0)
        out_rows, q_grad, k_sum, v_sum, logsum = per_head(query_part, key_part, val_part, grad_part, query_seg, key_seg, query_pos, key_pos)
        return (out_rows.reshape(TOK_DEV, -1), q_grad.reshape(TOK_DEV, -1), k_sum.reshape(window, -1),
                v_sum.reshape(window, -1), logsum.reshape(QUERY_HEADS, TOK_DEV))

    out_all, qg_all, k_all, v_all, lse_all = lax.map(one_shard, jnp.arange(N_DP, dtype=jnp.int32))
    attention_out = out_all.reshape(TOKEN_ROWS_ALL, QUERY_HEADS * HEAD_SIZE)
    query_grad = qg_all.reshape(TOKEN_ROWS_ALL, QUERY_HEADS * HEAD_SIZE)
    tail = TOK_DEV - reach_rows

    def combine(block):
        own = block[:, reach_rows:]
        from_next = jnp.concatenate([block[1:, :reach_rows], jnp.zeros_like(block[:1, :reach_rows])], axis=0)
        joined = jnp.concatenate([own[:, :tail], own[:, tail:] + from_next], axis=1)
        return joined.reshape(TOKEN_ROWS_ALL, KEY_VALUE_HEADS * HEAD_SIZE).astype(jnp.bfloat16)

    key_gradient = combine(k_all)
    value_gradient = combine(v_all)
    softmax_logsum = jnp.transpose(lse_all, (1, 0, 2)).reshape(QUERY_HEADS, TOKEN_ROWS_ALL)

    key_value_joined = jnp.stack([key_gradient.reshape(TOKEN_ROWS_ALL, KEY_VALUE_HEADS, HEAD_SIZE), value_gradient.reshape(TOKEN_ROWS_ALL, KEY_VALUE_HEADS, HEAD_SIZE)], axis=2).reshape(TOKEN_ROWS_ALL, 2 * KEY_VALUE_HEADS * HEAD_SIZE)

    def accumulate_shard(total, shard_id):
        first = (shard_id * TOK_DEV).astype(jnp.int32)
        input_part = lax.dynamic_slice_in_dim(inputs, first, TOK_DEV, 0)
        grad_part = lax.dynamic_slice_in_dim(key_value_joined, first, TOK_DEV, 0)
        partial_sum = jnp.dot(input_part.T, grad_part, preferred_element_type=jnp.float32).astype(jnp.bfloat16)
        partial_sum = lax.optimization_barrier(partial_sum)
        return total + partial_sum.astype(jnp.float32), None

    projection_weight_gradient, leftover_slots = lax.scan(accumulate_shard, jnp.zeros((MODEL_WIDTH, 2 * KEY_VALUE_HEADS * HEAD_SIZE), jnp.float32), jnp.arange(N_DP, dtype=jnp.int32))
    return attention_out, query_grad, key_gradient, value_gradient, softmax_logsum, projection_weight_gradient
```

```python
import jax
import jax.numpy as jnp
from jax import lax
from jax.experimental import pallas as pl
from jax.experimental.pallas import tpu as pltpu
from jax.sharding import PartitionSpec as P

HEAD = 128
REACH = 256
BLOCK = 128
WINDOW = REACH + BLOCK
NX, NY, NZ = 4, 4, 8
F32 = jnp.float32
BF16 = jnp.bfloat16
NT = (((1,), (1,)), ((), ()))
TN = (((0,), (0,)), ((), ()))


def dot(a, b, dims=(((1,), (0,)), ((), ()))):
    return lax.dot_general(a, b, dims, preferred_element_type=F32)


def attend_rows(q_ref, g_ref, k_lo, k_hi, v_lo, v_hi, sq_ref, sk_ref, o_ref, dq_ref, lse_ref, dk_ref, dv_ref, p_s, ds_s):
    heads = q_ref.shape[1] // HEAD
    scale = HEAD ** (-0.5)
    keys = jnp.concatenate([k_lo[...], k_hi[...]], axis=0)
    vals = jnp.concatenate([v_lo[...], v_hi[...]], axis=0)
    keys_t = keys.T
    vals_t = vals.T
    dk_ref[...] = jnp.zeros_like(dk_ref)
    dv_ref[...] = jnp.zeros_like(dv_ref)
    for j in range(REACH // BLOCK):
        lo = j * BLOCK
        rows = slice(lo, lo + BLOCK)
        win = slice(lo, lo + WINDOW)
        k_w, v_w = keys[win], vals[win]
        kt_w, vt_w = keys_t[:, win], vals_t[:, win]
        key_at = lax.broadcasted_iota(jnp.int32, (WINDOW, BLOCK), 0)
        query_at = lax.broadcasted_iota(jnp.int32, (WINDOW, BLOCK), 1) + REACH
        allowed = (sk_ref[win, :] == sq_ref[:, rows]) & (key_at <= query_at)
        bias = jnp.where(allowed, 0.0, -1e30).astype(F32)
        bias = jnp.concatenate([bias, bias], axis=1)
        q_parts, g_parts = [], []
        for h in range(0, heads, 2):
            c0 = slice(h * HEAD, (h + 1) * HEAD)
            c1 = slice((h + 1) * HEAD, (h + 2) * HEAD)
            qp = jnp.concatenate([q_ref[rows, c0], q_ref[rows, c1]], axis=0)
            gp = jnp.concatenate([g_ref[rows, c0], g_ref[rows, c1]], axis=0)
            q_parts.append(qp)
            g_parts.append(gp)
            s = dot(k_w, qp, NT) * scale + bias
            top = jnp.max(s, axis=0, keepdims=True)
            e = jnp.exp(s - top)
            total = jnp.sum(e, axis=0, keepdims=True)
            lse = top + jnp.log(total)
            lse_ref[h : h + 1, rows] = lse[:, :BLOCK]
            lse_ref[h + 1 : h + 2, rows] = lse[:, BLOCK:]
            p = e * (1.0 / total)
            dp = dot(v_w, gp, NT)
            delta = jnp.sum(p * dp, axis=0, keepdims=True)
            ds = (p * (dp - delta)).astype(BF16)
            p_low = p.astype(BF16)
            cols = slice(h * BLOCK, (h + 2) * BLOCK)
            p_s[:, cols] = p_low
            ds_s[:, cols] = ds
            o = dot(vt_w, p_low).T
            o_ref[rows, c0] = o[:BLOCK].astype(BF16)
            o_ref[rows, c1] = o[BLOCK:].astype(BF16)
            dq = (dot(kt_w, ds) * scale).T
            dq_ref[rows, c0] = dq[:BLOCK].astype(BF16)
            dq_ref[rows, c1] = dq[BLOCK:].astype(BF16)
        dv_ref[win, :] += dot(p_s[...], jnp.concatenate(g_parts, axis=0))
        dk_ref[win, :] += dot(ds_s[...], jnp.concatenate(q_parts, axis=0)) * scale


def late_kernel(q, g, k_lo, k_hi, v_lo, v_hi, sq, sk, o, dq, lse, dk_out, dv_out, p_s, ds_s):
    attend_rows(q, g, k_lo, k_hi, v_lo, v_hi, sq, sk, o, dq, lse, dk_out, dv_out, p_s, ds_s)


def early_kernel(q, g, k_lo, k_hi, v_lo, v_hi, sq, sk, dk_late, dv_late, o_in, dq_in, lse_in, o, dq, lse, joined, back, p_s, ds_s, dk, dv):
    attend_rows(q, g, k_lo, k_hi, v_lo, v_hi, sq, sk, o, dq, lse, dk, dv, p_s, ds_s)
    back[:, :HEAD] = dk[:REACH].astype(BF16)
    back[:, HEAD:] = dv[:REACH].astype(BF16)
    joined[:, :HEAD] = (dk[REACH:] + dk_late[...]).astype(BF16)
    joined[:, HEAD:] = (dv[REACH:] + dv_late[...]).astype(BF16)


def spec(shape, at):
    return pl.BlockSpec(shape, lambda i: at)


def attention(queries, out_grad, key_rows, value_matrix, prior, seg_own, seg_prior):
    tok, width = queries.shape
    heads = width // HEAD
    half = tok // 2
    seg_row = seg_own.reshape(1, tok)
    seg_col = seg_own.reshape(tok, 1)
    cost = pl.CostEstimate(flops=6 * 2 * half * WINDOW * width, bytes_accessed=4 << 20, transcendentals=half * WINDOW * heads)
    params = pltpu.CompilerParams(vmem_limit_bytes=48 << 20)
    wide = lambda i: spec((half, width), (i, 0))
    kv = lambda i: spec((half, HEAD), (i, 0))
    scratch = [pltpu.VMEM((WINDOW, heads * BLOCK), BF16)] * 2
    rows_out = jax.ShapeDtypeStruct((tok, width), BF16)
    lse_out = jax.ShapeDtypeStruct((heads, tok), F32)
    grad = jax.ShapeDtypeStruct((tok, HEAD), F32)
    o, dq, lse, dk_late, dv_late = pl.pallas_call(
        late_kernel,
        grid=(1,),
        in_specs=[wide(1), wide(1), kv(0), kv(1), kv(0), kv(1), spec((1, half), (0, 1)), spec((tok, 1), (0, 0))],
        out_specs=[wide(1), wide(1), spec((heads, half), (0, 1)), spec((tok, HEAD), (0, 0)), spec((tok, HEAD), (0, 0))],
        out_shape=[rows_out, rows_out, lse_out, grad, grad],
        scratch_shapes=scratch,
        cost_estimate=cost,
        compiler_params=params,
        name="attend_late",
    )(queries, out_grad, key_rows, key_rows, value_matrix, value_matrix, seg_row, seg_col)
    seg_col_early = jnp.concatenate([seg_prior.reshape(half, 1), seg_col[:half]], axis=0)
    hbm = pl.BlockSpec(memory_space=pl.ANY)
    pair = jax.ShapeDtypeStruct((half, 2 * HEAD), BF16)
    o, dq, lse, joined_low, back = pl.pallas_call(
        early_kernel,
        grid=(1,),
        in_specs=[wide(0), wide(0), kv(0), kv(0), spec((half, HEAD), (0, 1)), kv(0), spec((1, half), (0, 0)), spec((tok, 1), (0, 0)),
                  kv(0), kv(0), hbm, hbm, hbm],
        out_specs=[wide(0), wide(0), spec((heads, half), (0, 0)), spec((half, 2 * HEAD), (0, 0)), spec((half, 2 * HEAD), (0, 0))],
        out_shape=[rows_out, rows_out, lse_out, pair, pair],
        scratch_shapes=scratch + [pltpu.VMEM((tok, HEAD), F32)] * 2,
        input_output_aliases={10: 0, 11: 1, 12: 2},
        cost_estimate=cost,
        compiler_params=params,
        name="attend_early",
    )(queries, out_grad, prior, key_rows, prior, value_matrix, seg_row, seg_col_early, dk_late, dv_late, o, dq, lse)
    return o, dq, lse, joined_low, back, dk_late, dv_late


def weight_kernel(core, a0, a1, a3, a2l, a2h, b0, b1, b3, b2, c0, c1, c3, c2, out):
    mine = pl.ds(pl.multiple_of(core[0] * 2 * HEAD, 2 * HEAD), 2 * HEAD)
    other = pl.ds(pl.multiple_of((1 - core[0]) * 2 * HEAD, 2 * HEAD), 2 * HEAD)
    half = a2l.shape[0]
    for cols, (r0, r1, r3, r2) in ((mine, (b0, b1, b3, b2)), (other, (c0, c1, c3, c2))):
        total = dot(a0[...], r0[...], TN) + dot(a1[...], r1[...], TN) + dot(a3[...], r3[...], TN)
        total += dot(a2l[...], r2[:half], TN) + dot(a2h[...], r2[half:], TN)
        out[:, cols] = total.astype(BF16)


def weight_partial(core, a, b, c):
    tok, width = a[0].shape
    tile = 256
    col = lambda rows: pl.BlockSpec((rows, tile), lambda i, core: (0, i))
    whole = pl.BlockSpec((tok, 2 * HEAD), lambda i, core: (0, 0))
    return pl.pallas_call(
        weight_kernel,
        grid_spec=pltpu.PrefetchScalarGridSpec(
            num_scalar_prefetch=1,
            grid=(width // tile,),
            in_specs=[col(tok)] * 3 + [col(tok // 2)] * 2 + [whole] * 8,
            out_specs=pl.BlockSpec((tile, 4 * HEAD), lambda i, core: (i, 0)),
        ),
        out_shape=jax.ShapeDtypeStruct((width, 4 * HEAD), BF16),
        cost_estimate=pl.CostEstimate(flops=2 * width * 4 * HEAD * 4 * tok, bytes_accessed=8 << 20, transcendentals=0),
        compiler_params=pltpu.CompilerParams(vmem_limit_bytes=48 << 20),
        name="weight_partial",
    )(core, *a, *b, *c)


def sum_kernel(y, parts, out):
    width = parts.shape[2]
    for b in range(NX):
        x = lax.rem(b - y[0] + NX, NX)
        total = parts[x].astype(F32)
        for z in range(1, NZ):
            total += parts[z * NX + x].astype(F32)
        out[:, b * width : (b + 1) * width] = total


def sum_parts(y, parts):
    sources, rows, width = parts.shape
    return pl.pallas_call(
        sum_kernel,
        grid_spec=pltpu.PrefetchScalarGridSpec(
            num_scalar_prefetch=1,
            grid=(1,),
            in_specs=[pl.BlockSpec((sources, rows, width), lambda i, y: (0, 0, 0))],
            out_specs=pl.BlockSpec((rows, NX * width), lambda i, y: (0, 0)),
        ),
        out_shape=jax.ShapeDtypeStruct((rows, NX * width), F32),
        cost_estimate=pl.CostEstimate(flops=sources * rows * width, bytes_accessed=2 << 20, transcendentals=0),
        name="sum_parts",
    )(y, parts)


def along_x(steps):
    return [(z * NX + x, z * NX + (x + steps) % NX) for z in range(NZ) for x in range(NX)]


def to_columns(steps):
    pairs = []
    for z in range(NZ):
        for x in range(NX):
            for y in range(NY):
                for c in range(2):
                    x_to = (x + steps) % NX
                    y_to = (y - x_to) % NY
                    pairs.append((((z * NX + x) * NY + y) * 2 + c, ((z * NX + x_to) * NY + y_to) * 2 + c))
    return pairs


def body(queries, key_rows, value_matrix, out_grad, inputs, doc_ids):
    shard = lax.axis_index("dp")
    tensor = lax.axis_index("tensor")
    tok = queries.shape[0]
    half = tok // 2
    shards = lax.axis_size("dp")
    first = shard * tok
    seg_own = lax.dynamic_slice_in_dim(doc_ids, first, tok)
    seg_prior = jnp.where(shard > 0, lax.dynamic_slice_in_dim(doc_ids, jnp.maximum(first - half, 0), half), -1)
    tail = jnp.concatenate([key_rows[half:], value_matrix[half:]], axis=1)
    prior = lax.ppermute(tail, "dp", [(i, i + 1) for i in range(shards - 1)])

    in_left = lax.ppermute(inputs, "dp", along_x(1))
    in_right = lax.ppermute(inputs, "dp", along_x(-1))
    in_far_low = lax.ppermute(in_left[:half], "dp", along_x(1))
    in_far_high = lax.ppermute(in_right[half:], "dp", along_x(-1))

    out_rows, query_grad, logsum, joined_low, back, dk_late, dv_late = attention(
        queries, out_grad, key_rows, value_matrix, prior, seg_own, seg_prior
    )
    back = lax.ppermute(back, "dp", [(i + 1, i) for i in range(shards - 1)])
    late = jnp.concatenate([dk_late[half:], dv_late[half:]], axis=1)
    joined_high = (late + back.astype(F32)).astype(BF16)
    joined = jnp.concatenate([joined_low, joined_high], axis=0)
    key_gradient = joined[:, :HEAD]
    value_gradient = joined[:, HEAD:]

    order = (0, 1, 3, 2)
    mine = [lax.ppermute(joined, ("dp", "tensor"), to_columns(d)) for d in order]
    swap = [(t, t ^ 1) for t in range(2 * NY)]
    other = [lax.ppermute(m, "tensor", swap) for m in mine]
    core = (tensor % 2).astype(jnp.int32).reshape(1)
    partial = weight_partial(core, (inputs, in_left, in_right, in_far_low, in_far_high), mine, other)
    parts = lax.all_to_all(partial, "dp", 0, 0, tiled=True)
    row = (tensor // 2).astype(jnp.int32).reshape(1)
    weight_grad = sum_parts(row, parts.reshape(shards, -1, 4 * HEAD))
    return out_rows, query_grad, key_gradient, value_gradient, logsum, weight_grad


def solution(mesh):
    split = P("dp", "tensor")
    return jax.shard_map(
        body,
        mesh=mesh,
        in_specs=(split, split, split, split, split, P()),
        out_specs=(split, split, split, split, P("tensor", "dp"), P(("tensor", "dp"), None)),
        check_vma=False,
    )
```

```python
import jax
import jax.numpy as jnp
from jax import lax
from jax.experimental import pallas as pl
from jax.experimental.pallas import tpu as pltpu
from jax.sharding import PartitionSpec as P

HEAD = 128
REACH = 256
BLOCK = 128
WINDOW = REACH + BLOCK
NX, NY, NZ = 4, 4, 8
ORDER = (0, 1, 3, 2)
F32 = jnp.float32
BF16 = jnp.bfloat16
NT = (((1,), (1,)), ((), ()))
TN = (((0,), (0,)), ((), ()))


def dot(a, b, dims=(((1,), (0,)), ((), ()))):
    return lax.dot_general(a, b, dims, preferred_element_type=F32)


def attend_rows(q_ref, g_ref, k_lo, k_hi, v_lo, v_hi, doc_ref, first, o_ref, dq_ref, lse_ref, dk_ref, dv_ref, p_s, ds_s):
    heads = q_ref.shape[1] // HEAD
    scale = HEAD ** (-0.5)
    keys = jnp.concatenate([k_lo[...], k_hi[...]], axis=0)
    vals = jnp.concatenate([v_lo[...], v_hi[...]], axis=0)
    docs = [doc_ref[pl.ds(jnp.maximum(first + b, 0), 1), :].astype(F32) for b in range((2 * REACH) // BLOCK)]
    docs = [jnp.broadcast_to(jnp.where(first + b >= 0, d, -1.0), (BLOCK, BLOCK)) for b, d in enumerate(docs)]
    docs_t = [d.T for d in docs]
    keys_t = keys.T
    vals_t = vals.T
    dk_ref[...] = jnp.zeros_like(dk_ref)
    dv_ref[...] = jnp.zeros_like(dv_ref)
    for j in range(REACH // BLOCK):
        lo = j * BLOCK
        rows = slice(lo, lo + BLOCK)
        win = slice(lo, lo + WINDOW)
        k_w, v_w = keys[win], vals[win]
        kt_w, vt_w = keys_t[:, win], vals_t[:, win]
        key_at = lax.broadcasted_iota(jnp.int32, (WINDOW, BLOCK), 0)
        query_at = lax.broadcasted_iota(jnp.int32, (WINDOW, BLOCK), 1) + REACH
        own = docs[j + REACH // BLOCK]
        same = jnp.concatenate([jnp.where(d == own, 1.0, 0.0) for d in docs_t[j : j + WINDOW // BLOCK]], axis=0)
        allowed = (same > 0.5) & (key_at <= query_at)
        bias = jnp.where(allowed, 0.0, -1e30).astype(F32)
        bias = jnp.concatenate([bias, bias], axis=1)
        q_parts, g_parts = [], []
        for h in range(0, heads, 2):
            c0 = slice(h * HEAD, (h + 1) * HEAD)
            c1 = slice((h + 1) * HEAD, (h + 2) * HEAD)
            qp = jnp.concatenate([q_ref[rows, c0], q_ref[rows, c1]], axis=0)
            gp = jnp.concatenate([g_ref[rows, c0], g_ref[rows, c1]], axis=0)
            q_parts.append(qp)
            g_parts.append(gp)
            s = dot(k_w, qp, NT) * scale + bias
            top = jnp.max(s, axis=0, keepdims=True)
            e = jnp.exp(s - top)
            total = jnp.sum(e, axis=0, keepdims=True)
            lse = top + jnp.log(total)
            lse_ref[h : h + 1, rows] = lse[:, :BLOCK]
            lse_ref[h + 1 : h + 2, rows] = lse[:, BLOCK:]
            p = e * (1.0 / total)
            dp = dot(v_w, gp, NT)
            delta = jnp.sum(p * dp, axis=0, keepdims=True)
            ds = (p * (dp - delta)).astype(BF16)
            p_low = p.astype(BF16)
            cols = slice(h * BLOCK, (h + 2) * BLOCK)
            p_s[:, cols] = p_low
            ds_s[:, cols] = ds
            o = dot(vt_w, p_low).T
            o_ref[rows, c0] = o[:BLOCK].astype(BF16)
            o_ref[rows, c1] = o[BLOCK:].astype(BF16)
            dq = (dot(kt_w, ds) * scale).T
            dq_ref[rows, c0] = dq[:BLOCK].astype(BF16)
            dq_ref[rows, c1] = dq[BLOCK:].astype(BF16)
        dv_ref[win, :] += dot(p_s[...], jnp.concatenate(g_parts, axis=0))
        dk_ref[win, :] += dot(ds_s[...], jnp.concatenate(q_parts, axis=0)) * scale


def early_kernel(q, g, k_lo, k_hi, v_lo, v_hi, doc, o, dq, lse, dk_own, dv_own, back, p_s, ds_s, dk, dv):
    first = lax.axis_index("dp") * (2 * REACH // BLOCK) - REACH // BLOCK
    attend_rows(q, g, k_lo, k_hi, v_lo, v_hi, doc, first, o, dq, lse, dk, dv, p_s, ds_s)
    back[:, :HEAD] = dk[:REACH].astype(BF16)
    back[:, HEAD:] = dv[:REACH].astype(BF16)
    dk_own[...] = dk[REACH:]
    dv_own[...] = dv[REACH:]


def late_kernel(q, g, k_lo, k_hi, v_lo, v_hi, doc, dk_own, dv_own, o_in, dq_in, lse_in, o, dq, lse, low, high, p_s, ds_s, dk, dv):
    first = lax.axis_index("dp") * (2 * REACH // BLOCK)
    attend_rows(q, g, k_lo, k_hi, v_lo, v_hi, doc, first, o, dq, lse, dk, dv, p_s, ds_s)
    low[:, :HEAD] = (dk[:REACH] + dk_own[...]).astype(BF16)
    low[:, HEAD:] = (dv[:REACH] + dv_own[...]).astype(BF16)
    high[:, :HEAD] = dk[REACH:]
    high[:, HEAD:] = dv[REACH:]


def spec(shape, at):
    return pl.BlockSpec(shape, lambda i: at)


def attention(queries, out_grad, key_rows, value_matrix, prior_keys, prior_vals, docs):
    tok, width = queries.shape
    heads = width // HEAD
    half = tok // 2
    cost = pl.CostEstimate(flops=6 * 2 * half * WINDOW * width, bytes_accessed=32 << 20, transcendentals=half * WINDOW * heads)
    params = pltpu.CompilerParams(vmem_limit_bytes=60 << 20)
    wide = lambda i: spec((half, width), (i, 0))
    kv = lambda i: spec((half, HEAD), (i, 0))
    doc = spec(docs.shape, (0, 0))
    scratch = [pltpu.VMEM((WINDOW, heads * BLOCK), BF16)] * 2 + [pltpu.VMEM((tok, HEAD), F32)] * 2
    rows_out = jax.ShapeDtypeStruct((tok, width), BF16)
    lse_out = jax.ShapeDtypeStruct((heads, tok), F32)
    grad = jax.ShapeDtypeStruct((half, HEAD), F32)
    part = spec((half, HEAD), (0, 0))
    pair = spec((half, 2 * HEAD), (0, 0))
    o, dq, lse, dk_own, dv_own, back = pl.pallas_call(
        early_kernel,
        grid=(1,),
        in_specs=[wide(0), wide(0), kv(1), kv(0), kv(1), kv(0), doc],
        out_specs=[wide(0), wide(0), spec((heads, half), (0, 0)), part, part, pair],
        out_shape=[rows_out, rows_out, lse_out, grad, grad, jax.ShapeDtypeStruct((half, 2 * HEAD), BF16)],
        scratch_shapes=scratch,
        cost_estimate=cost,
        compiler_params=params,
        name="attend_early",
    )(queries, out_grad, prior_keys, key_rows, prior_vals, value_matrix, docs)
    hbm = pl.BlockSpec(memory_space=pl.ANY)
    o, dq, lse, low, high = pl.pallas_call(
        late_kernel,
        grid=(1,),
        in_specs=[wide(1), wide(1), kv(0), kv(1), kv(0), kv(1), doc, part, part, hbm, hbm, hbm],
        out_specs=[wide(1), wide(1), spec((heads, half), (0, 1)), pair, pair],
        out_shape=[rows_out, rows_out, lse_out, jax.ShapeDtypeStruct((half, 2 * HEAD), BF16), jax.ShapeDtypeStruct((half, 2 * HEAD), F32)],
        scratch_shapes=scratch,
        input_output_aliases={9: 0, 10: 1, 11: 2},
        cost_estimate=cost,
        compiler_params=params,
        name="attend_late",
    )(queries, out_grad, key_rows, key_rows, value_matrix, value_matrix, docs, dk_own, dv_own, o, dq, lse)
    return o, dq, lse, back, low, high, dk_own


def split_kernel(x, first, second):
    half = first.shape[1]
    first[...] = x[:, :half]
    second[...] = x[:, half:]


def split_inputs(inputs):
    tok, width = inputs.shape
    part = jax.ShapeDtypeStruct((tok, width // 2), BF16)
    return pl.pallas_call(
        split_kernel,
        grid=(1,),
        in_specs=[spec((tok, width), (0, 0))],
        out_specs=[spec((tok, width // 2), (0, 0))] * 2,
        out_shape=[part, part],
        compiler_params=pltpu.CompilerParams(vmem_limit_bytes=48 << 20),
        name="split_inputs",
    )(inputs)


def join_kernel(low, high, back, joined, key_grad, value_grad):
    half = low.shape[0]
    rest = (high[...] + back[...].astype(F32)).astype(BF16)
    joined[:half] = low[...]
    joined[half:] = rest
    key_grad[:half] = low[:, :HEAD]
    key_grad[half:] = rest[:, :HEAD]
    value_grad[:half] = low[:, HEAD:]
    value_grad[half:] = rest[:, HEAD:]


def join_gradients(low, high, back):
    half, width = low.shape
    part = spec((half, width), (0, 0))
    shapes = [(2 * half, width), (2 * half, HEAD), (2 * half, HEAD)]
    return pl.pallas_call(
        join_kernel,
        grid=(1,),
        in_specs=[part] * 3,
        out_specs=[spec(shape, (0, 0)) for shape in shapes],
        out_shape=[jax.ShapeDtypeStruct(shape, BF16) for shape in shapes],
        name="join_gradients",
    )(low, high, back)


def weight_kernel(a0, a1, a3, a2, d0, d1, d3, d2, b0, b1, b3, b2, c0, c1, c3, c2, out):
    core = lax.rem(lax.axis_index("tensor"), 2)
    mine = pl.ds(pl.multiple_of(core * 2 * HEAD, 2 * HEAD), 2 * HEAD)
    other = pl.ds(pl.multiple_of((1 - core) * 2 * HEAD, 2 * HEAD), 2 * HEAD)

    def multiply(left):
        for cols, right in ((mine, (b0, b1, b3, b2)), (other, (c0, c1, c3, c2))):
            total = dot(left[0][...], right[0][...], TN)
            for l, r in zip(left[1:], right[1:]):
                total += dot(l[...], r[...], TN)
            out[:, cols] = total.astype(BF16)

    steps = pl.num_programs(0) // 2

    @pl.when(pl.program_id(0) < steps)
    def _():
        multiply((a0, a1, a3, a2))

    @pl.when(pl.program_id(0) >= steps)
    def _():
        multiply((d0, d1, d3, d2))


def weight_partial(first, second, mine, other):
    tile = 2 * HEAD
    tok, width = first[0].shape
    steps = width // tile
    low = pl.BlockSpec((tok, tile), lambda i: (0, jnp.minimum(i, steps - 1)))
    high = pl.BlockSpec((tok, tile), lambda i: (0, jnp.maximum(i - steps, 0)))
    whole = pl.BlockSpec((tok, 2 * HEAD), lambda i: (0, 0))
    return pl.pallas_call(
        weight_kernel,
        grid=(2 * steps,),
        in_specs=[low] * 4 + [high] * 4 + [whole] * 8,
        out_specs=pl.BlockSpec((tile, 4 * HEAD), lambda i: (i, 0)),
        out_shape=jax.ShapeDtypeStruct((2 * width, 4 * HEAD), BF16),
        cost_estimate=pl.CostEstimate(flops=4 * width * 4 * HEAD * 4 * tok, bytes_accessed=8 << 20, transcendentals=0),
        compiler_params=pltpu.CompilerParams(vmem_limit_bytes=60 << 20),
        name="weight_partial",
    )(*first, *second, *mine, *other)


def sum_kernel(parts, out):
    y = lax.axis_index("tensor") // 2
    wide = 2 * HEAD
    for head in range(2 * NX):
        x = lax.rem(head // 2 - y + NX + 2 * (head % 2), NX)
        side = slice((head % 2) * wide, (head % 2 + 1) * wide)
        total = parts[x, :, side].astype(F32)
        for z in range(1, NZ):
            total += parts[z * NX + x, :, side].astype(F32)
        out[:, head * wide : (head + 1) * wide] = total


def sum_parts(parts):
    sources, rows, width = parts.shape
    return pl.pallas_call(
        sum_kernel,
        grid=(1,),
        in_specs=[spec((sources, rows, width), (0, 0, 0))],
        out_specs=spec((rows, NX * width), (0, 0)),
        out_shape=jax.ShapeDtypeStruct((rows, NX * width), F32),
        cost_estimate=pl.CostEstimate(flops=sources * rows * width, bytes_accessed=2 << 20, transcendentals=0),
        compiler_params=pltpu.CompilerParams(vmem_limit_bytes=60 << 20),
        name="sum_parts",
    )(parts)


def along_x(steps):
    return [(z * NX + x, z * NX + (x + steps) % NX) for z in range(NZ) for x in range(NX)]


def to_columns(steps):
    pairs = []
    for z in range(NZ):
        for x in range(NX):
            for y in range(NY):
                for c in range(2):
                    x_to = (x + steps) % NX
                    y_to = (y - x_to - 2 * c) % NY
                    pairs.append((((z * NX + x) * NY + y) * 2 + c, ((z * NX + x_to) * NY + y_to) * 2 + c))
    return pairs


def after(value, *others):
    return lax.optimization_barrier((value, *others))[0]


def body(queries, key_rows, value_matrix, out_grad, inputs, doc_ids):
    shards = lax.axis_size("dp")
    docs = doc_ids.reshape(-1, BLOCK)
    onward = [(i, i + 1) for i in range(shards - 1)]
    backward = [(i + 1, i) for i in range(shards - 1)]
    prior_keys = lax.ppermute(key_rows, "dp", onward)
    prior_vals = lax.ppermute(value_matrix, "dp", onward)

    first, second = split_inputs(inputs)
    first_sent = after(first, prior_keys, prior_vals)
    first_left = lax.ppermute(first_sent, "dp", along_x(1))
    first_right = lax.ppermute(first_sent, "dp", along_x(-1))

    out_rows, query_grad, logsum, back, low, high, dk_early = attention(
        queries, out_grad, key_rows, value_matrix, prior_keys, prior_vals, docs
    )
    second_left = lax.ppermute(after(second, dk_early), "dp", along_x(1))
    back = lax.ppermute(back, "dp", backward)
    second_right = lax.ppermute(after(second, back), "dp", along_x(-1))
    first_far = lax.ppermute(after(first_left, low), "dp", along_x(1))
    second_far = lax.ppermute(second_right, "dp", along_x(-1))
    joined, key_gradient, value_gradient = join_gradients(low, high, after(back, first_right, first_left))

    mine = [lax.ppermute(joined, ("dp", "tensor"), to_columns(d)) for d in ORDER]
    swap = [(t, t ^ 1) for t in range(2 * NY)]
    other = [lax.ppermute(m, "tensor", swap) for m in mine]
    first_all = (first, first_left, first_right, first_far)
    second_all = (second, second_left, second_right, second_far)
    partial = weight_partial(first_all, second_all, mine, other)
    parts = lax.all_to_all(partial, "dp", 0, 0, tiled=True)
    weight_grad = sum_parts(parts.reshape(shards, -1, 4 * HEAD))
    return out_rows, query_grad, key_gradient, value_gradient, logsum, weight_grad


def solution(mesh):
    split = P("dp", "tensor")
    return jax.shard_map(
        body,
        mesh=mesh,
        in_specs=(split, split, split, split, split, P()),
        out_specs=(split, split, split, split, P("tensor", "dp"), P(("tensor", "dp"), None)),
        check_vma=False,
    )
```

```python
import jax
import jax.numpy as jnp
from jax import lax
from jax.experimental import pallas as pl
from jax.experimental.pallas import tpu as pltpu
from jax.sharding import PartitionSpec as P

HEAD = 128
REACH = 256
BLOCK = 128
WINDOW = REACH + BLOCK
NX, NY, NZ = 4, 4, 8
ORDER = (0, 1, 3, 2)
F32 = jnp.float32
BF16 = jnp.bfloat16
NT = (((1,), (1,)), ((), ()))
TN = (((0,), (0,)), ((), ()))


def dot(a, b, dims=(((1,), (0,)), ((), ()))):
    return lax.dot_general(a, b, dims, preferred_element_type=F32)


def attend_rows(q_ref, g_ref, k_lo, k_hi, v_lo, v_hi, doc_ref, first, o_ref, dq_ref, lse_ref, dk_ref, dv_ref, p_s, ds_s):
    heads = q_ref.shape[1] // HEAD
    scale = HEAD ** (-0.5)
    keys = jnp.concatenate([k_lo[...], k_hi[...]], axis=0)
    vals = jnp.concatenate([v_lo[...], v_hi[...]], axis=0)
    docs = [doc_ref[pl.ds(jnp.maximum(first + b, 0), 1), :].astype(F32) for b in range((2 * REACH) // BLOCK)]
    docs = [jnp.broadcast_to(jnp.where(first + b >= 0, d, -1.0), (BLOCK, BLOCK)) for b, d in enumerate(docs)]
    docs_t = [d.T for d in docs]
    keys_t = keys.T
    vals_t = vals.T
    dk_ref[...] = jnp.zeros_like(dk_ref)
    dv_ref[...] = jnp.zeros_like(dv_ref)
    for j in range(REACH // BLOCK):
        lo = j * BLOCK
        rows = slice(lo, lo + BLOCK)
        win = slice(lo, lo + WINDOW)
        k_w, v_w = keys[win], vals[win]
        kt_w, vt_w = keys_t[:, win], vals_t[:, win]
        key_at = lax.broadcasted_iota(jnp.int32, (WINDOW, BLOCK), 0)
        query_at = lax.broadcasted_iota(jnp.int32, (WINDOW, BLOCK), 1) + REACH
        own = docs[j + REACH // BLOCK]
        same = jnp.concatenate([jnp.where(d == own, 1.0, 0.0) for d in docs_t[j : j + WINDOW // BLOCK]], axis=0)
        allowed = (same > 0.5) & (key_at <= query_at)
        bias = jnp.where(allowed, 0.0, -1e30).astype(F32)
        bias = jnp.concatenate([bias, bias], axis=1)
        q_parts, g_parts = [], []
        for h in range(0, heads, 2):
            c0 = slice(h * HEAD, (h + 1) * HEAD)
            c1 = slice((h + 1) * HEAD, (h + 2) * HEAD)
            qp = jnp.concatenate([q_ref[rows, c0], q_ref[rows, c1]], axis=0)
            gp = jnp.concatenate([g_ref[rows, c0], g_ref[rows, c1]], axis=0)
            q_parts.append(qp)
            g_parts.append(gp)
            s = dot(k_w, qp, NT) * scale + bias
            top = jnp.max(s, axis=0, keepdims=True)
            e = jnp.exp(s - top)
            total = jnp.sum(e, axis=0, keepdims=True)
            lse = top + jnp.log(total)
            lse_ref[h : h + 1, rows] = lse[:, :BLOCK]
            lse_ref[h + 1 : h + 2, rows] = lse[:, BLOCK:]
            p = e * (1.0 / total)
            dp = dot(v_w, gp, NT)
            delta = jnp.sum(p * dp, axis=0, keepdims=True)
            ds = (p * (dp - delta)).astype(BF16)
            p_low = p.astype(BF16)
            cols = slice(h * BLOCK, (h + 2) * BLOCK)
            p_s[:, cols] = p_low
            ds_s[:, cols] = ds
            o = dot(vt_w, p_low).T
            o_ref[rows, c0] = o[:BLOCK].astype(BF16)
            o_ref[rows, c1] = o[BLOCK:].astype(BF16)
            dq = (dot(kt_w, ds) * scale).T
            dq_ref[rows, c0] = dq[:BLOCK].astype(BF16)
            dq_ref[rows, c1] = dq[BLOCK:].astype(BF16)
        dv_ref[win, :] += dot(p_s[...], jnp.concatenate(g_parts, axis=0))
        dk_ref[win, :] += dot(ds_s[...], jnp.concatenate(q_parts, axis=0)) * scale


def early_kernel(q, g, k_lo, k_hi, v_lo, v_hi, doc, o, dq, lse, dk_own, dv_own, back, p_s, ds_s, dk, dv):
    first = lax.axis_index("dp") * (2 * REACH // BLOCK) - REACH // BLOCK
    attend_rows(q, g, k_lo, k_hi, v_lo, v_hi, doc, first, o, dq, lse, dk, dv, p_s, ds_s)
    back[:, :HEAD] = dk[:REACH].astype(BF16)
    back[:, HEAD:] = dv[:REACH].astype(BF16)
    dk_own[...] = dk[REACH:]
    dv_own[...] = dv[REACH:]


def late_kernel(q, g, k_lo, k_hi, v_lo, v_hi, doc, dk_own, dv_own, o_in, dq_in, lse_in, o, dq, lse, low, high, p_s, ds_s, dk, dv):
    first = lax.axis_index("dp") * (2 * REACH // BLOCK)
    attend_rows(q, g, k_lo, k_hi, v_lo, v_hi, doc, first, o, dq, lse, dk, dv, p_s, ds_s)
    low[:, :HEAD] = (dk[:REACH] + dk_own[...]).astype(BF16)
    low[:, HEAD:] = (dv[:REACH] + dv_own[...]).astype(BF16)
    high[:, :HEAD] = dk[REACH:]
    high[:, HEAD:] = dv[REACH:]


def spec(shape, at):
    return pl.BlockSpec(shape, lambda i: at)


def attention(queries, out_grad, key_rows, value_matrix, prior, docs):
    tok, width = queries.shape
    heads = width // HEAD
    half = tok // 2
    cost = pl.CostEstimate(flops=6 * 2 * half * WINDOW * width, bytes_accessed=32 << 20, transcendentals=half * WINDOW * heads)
    params = pltpu.CompilerParams(vmem_limit_bytes=60 << 20)
    wide = lambda i: spec((half, width), (i, 0))
    kv = lambda i: spec((half, HEAD), (i, 0))
    doc = spec(docs.shape, (0, 0))
    scratch = [pltpu.VMEM((WINDOW, heads * BLOCK), BF16)] * 2 + [pltpu.VMEM((tok, HEAD), F32)] * 2
    rows_out = jax.ShapeDtypeStruct((tok, width), BF16)
    lse_out = jax.ShapeDtypeStruct((heads, tok), F32)
    grad = jax.ShapeDtypeStruct((half, HEAD), F32)
    part = spec((half, HEAD), (0, 0))
    pair = spec((half, 2 * HEAD), (0, 0))
    o, dq, lse, dk_own, dv_own, back = pl.pallas_call(
        early_kernel,
        grid=(1,),
        in_specs=[wide(0), wide(0), kv(0), kv(0), spec((half, HEAD), (0, 1)), kv(0), doc],
        out_specs=[wide(0), wide(0), spec((heads, half), (0, 0)), part, part, pair],
        out_shape=[rows_out, rows_out, lse_out, grad, grad, jax.ShapeDtypeStruct((half, 2 * HEAD), BF16)],
        scratch_shapes=scratch,
        cost_estimate=cost,
        compiler_params=params,
        name="attend_early",
    )(queries, out_grad, prior, key_rows, prior, value_matrix, docs)
    hbm = pl.BlockSpec(memory_space=pl.ANY)
    o, dq, lse, low, high = pl.pallas_call(
        late_kernel,
        grid=(1,),
        in_specs=[wide(1), wide(1), kv(0), kv(1), kv(0), kv(1), doc, part, part, hbm, hbm, hbm],
        out_specs=[wide(1), wide(1), spec((heads, half), (0, 1)), pair, pair],
        out_shape=[rows_out, rows_out, lse_out, jax.ShapeDtypeStruct((half, 2 * HEAD), BF16), jax.ShapeDtypeStruct((half, 2 * HEAD), F32)],
        scratch_shapes=scratch,
        input_output_aliases={9: 0, 10: 1, 11: 2},
        cost_estimate=cost,
        compiler_params=params,
        name="attend_late",
    )(queries, out_grad, key_rows, key_rows, value_matrix, value_matrix, docs, dk_own, dv_own, o, dq, lse)
    return o, dq, lse, back, low, high, dk_own


def tail_kernel(k, v, out):
    out[:, :HEAD] = k[...]
    out[:, HEAD:] = v[...]


def pack_tail(key_rows, value_matrix):
    half = key_rows.shape[0] // 2
    return pl.pallas_call(
        tail_kernel,
        grid=(1,),
        in_specs=[spec((half, HEAD), (1, 0))] * 2,
        out_specs=spec((half, 2 * HEAD), (0, 0)),
        out_shape=jax.ShapeDtypeStruct((half, 2 * HEAD), BF16),
        name="pack_tail",
    )(key_rows, value_matrix)


def split_kernel(x, first, second):
    half = first.shape[0]
    first[...] = x[:, :half].T
    second[...] = x[:, half:].T


def split_inputs(inputs):
    tok, width = inputs.shape
    shape = (width // 2, tok)
    part = jax.ShapeDtypeStruct(shape, BF16)
    return pl.pallas_call(
        split_kernel,
        grid=(1,),
        in_specs=[spec((tok, width), (0, 0))],
        out_specs=[spec(shape, (0, 0))] * 2,
        out_shape=[part, part],
        compiler_params=pltpu.CompilerParams(vmem_limit_bytes=48 << 20),
        name="split_inputs",
    )(inputs)


def join_kernel(low, high, back, joined, key_grad, value_grad):
    half = low.shape[0]
    rest = (high[...] + back[...].astype(F32)).astype(BF16)
    joined[:half] = low[...]
    joined[half:] = rest
    key_grad[:half] = low[:, :HEAD]
    key_grad[half:] = rest[:, :HEAD]
    value_grad[:half] = low[:, HEAD:]
    value_grad[half:] = rest[:, HEAD:]


def join_gradients(low, high, back):
    half, width = low.shape
    part = spec((half, width), (0, 0))
    shapes = [(2 * half, width), (2 * half, HEAD), (2 * half, HEAD)]
    return pl.pallas_call(
        join_kernel,
        grid=(1,),
        in_specs=[part] * 3,
        out_specs=[spec(shape, (0, 0)) for shape in shapes],
        out_shape=[jax.ShapeDtypeStruct(shape, BF16) for shape in shapes],
        name="join_gradients",
    )(low, high, back)


def weight_kernel(a0, a1, a3, a2, d0, d1, d3, d2, b0, b1, b3, b2, c0, c1, c3, c2, out):
    core = lax.rem(lax.axis_index("tensor"), 2)
    mine = pl.ds(pl.multiple_of(core * 2 * HEAD, 2 * HEAD), 2 * HEAD)
    other = pl.ds(pl.multiple_of((1 - core) * 2 * HEAD, 2 * HEAD), 2 * HEAD)

    def multiply(left):
        right = [jnp.concatenate([b[...], c[...]], axis=1) for b, c in zip((b0, b1, b3, b2), (c0, c1, c3, c2))]
        total = dot(jnp.concatenate([l[...] for l in left], axis=1), jnp.concatenate(right, axis=0))
        out[:, mine] = total[:, : 2 * HEAD].astype(BF16)
        out[:, other] = total[:, 2 * HEAD :].astype(BF16)

    steps = pl.num_programs(0) // 2

    @pl.when(pl.program_id(0) < steps)
    def _():
        multiply((a0, a1, a3, a2))

    @pl.when(pl.program_id(0) >= steps)
    def _():
        multiply((d0, d1, d3, d2))


def weight_partial(first, second, mine, other):
    tile = 4 * HEAD
    width, tok = first[0].shape
    steps = width // tile
    low = pl.BlockSpec((tile, tok), lambda i: (jnp.minimum(i, steps - 1), 0))
    high = pl.BlockSpec((tile, tok), lambda i: (jnp.maximum(i - steps, 0), 0))
    whole = pl.BlockSpec((tok, 2 * HEAD), lambda i: (0, 0))
    return pl.pallas_call(
        weight_kernel,
        grid=(2 * steps,),
        in_specs=[low] * 4 + [high] * 4 + [whole] * 8,
        out_specs=pl.BlockSpec((tile, 4 * HEAD), lambda i: (i, 0)),
        out_shape=jax.ShapeDtypeStruct((2 * width, 4 * HEAD), BF16),
        cost_estimate=pl.CostEstimate(flops=4 * width * 4 * HEAD * 4 * tok, bytes_accessed=8 << 20, transcendentals=0),
        compiler_params=pltpu.CompilerParams(vmem_limit_bytes=60 << 20),
        name="weight_partial",
    )(*first, *second, *mine, *other)


def sum_kernel(parts, out):
    y = lax.axis_index("tensor") // 2
    wide = 2 * HEAD
    for head in range(2 * NX):
        x = lax.rem(head // 2 - y + NX + 2 * (head % 2), NX)
        side = slice((head % 2) * wide, (head % 2 + 1) * wide)
        total = parts[x, :, side].astype(F32)
        for z in range(1, NZ):
            total += parts[z * NX + x, :, side].astype(F32)
        out[:, head * wide : (head + 1) * wide] = total


def sum_parts(parts):
    sources, rows, width = parts.shape
    return pl.pallas_call(
        sum_kernel,
        grid=(1,),
        in_specs=[spec((sources, rows, width), (0, 0, 0))],
        out_specs=spec((rows, NX * width), (0, 0)),
        out_shape=jax.ShapeDtypeStruct((rows, NX * width), F32),
        cost_estimate=pl.CostEstimate(flops=sources * rows * width, bytes_accessed=2 << 20, transcendentals=0),
        compiler_params=pltpu.CompilerParams(vmem_limit_bytes=60 << 20),
        name="sum_parts",
    )(parts)


def along_x(steps):
    return [(z * NX + x, z * NX + (x + steps) % NX) for z in range(NZ) for x in range(NX)]


def to_columns(steps):
    pairs = []
    for z in range(NZ):
        for x in range(NX):
            for y in range(NY):
                for c in range(2):
                    x_to = (x + steps) % NX
                    y_to = (y - x_to - 2 * c) % NY
                    pairs.append((((z * NX + x) * NY + y) * 2 + c, ((z * NX + x_to) * NY + y_to) * 2 + c))
    return pairs


def after(value, *others):
    return lax.optimization_barrier((value, *others))[0]


def body(queries, key_rows, value_matrix, out_grad, inputs, doc_ids):
    shards = lax.axis_size("dp")
    docs = doc_ids.reshape(-1, BLOCK)
    onward = [(i, i + 1) for i in range(shards - 1)]
    backward = [(i + 1, i) for i in range(shards - 1)]
    prior = lax.ppermute(pack_tail(key_rows, value_matrix), "dp", onward)

    first, second = split_inputs(inputs)
    first_sent = after(first, prior)
    first_left = lax.ppermute(first_sent, "dp", along_x(1))
    first_right = lax.ppermute(first_sent, "dp", along_x(-1))

    out_rows, query_grad, logsum, back, low, high, dk_early = attention(
        queries, out_grad, key_rows, value_matrix, prior, docs
    )
    second_left = lax.ppermute(after(second, dk_early), "dp", along_x(1))
    back = lax.ppermute(back, "dp", backward)
    second_right = lax.ppermute(after(second, back), "dp", along_x(-1))
    first_far = lax.ppermute(after(first_left, low), "dp", along_x(1))
    second_far = lax.ppermute(second_right, "dp", along_x(-1))
    joined, key_gradient, value_gradient = join_gradients(low, high, after(back, first_right, first_left))

    mine = [lax.ppermute(joined, ("dp", "tensor"), to_columns(d)) for d in ORDER]
    swap = [(t, t ^ 1) for t in range(2 * NY)]
    other = [lax.ppermute(m, "tensor", swap) for m in mine]
    first_all = (first, first_left, first_right, first_far)
    second_all = (second, second_left, second_right, second_far)
    partial = weight_partial(first_all, second_all, mine, other)
    parts = lax.all_to_all(partial, "dp", 0, 0, tiled=True)
    weight_grad = sum_parts(parts.reshape(shards, -1, 4 * HEAD))
    return out_rows, query_grad, key_gradient, value_gradient, logsum, weight_grad


def solution(mesh):
    split = P("dp", "tensor")
    return jax.shard_map(
        body,
        mesh=mesh,
        in_specs=(split, split, split, split, split, P()),
        out_specs=(split, split, split, split, P("tensor", "dp"), P(("tensor", "dp"), None)),
        check_vma=False,
    )
```

```python
import jax
import jax.numpy as jnp
from jax import lax
from jax.experimental import pallas as pl
from jax.experimental.pallas import tpu as pltpu
from jax.sharding import PartitionSpec as P

HEAD = 128
REACH = 256
BLOCK = 128
WINDOW = REACH + BLOCK
NX, NY, NZ = 4, 4, 8
ORDER = (0, 1, 3, 2)
F32 = jnp.float32
BF16 = jnp.bfloat16
NT = (((1,), (1,)), ((), ()))
TN = (((0,), (0,)), ((), ()))


def dot(a, b, dims=(((1,), (0,)), ((), ()))):
    return lax.dot_general(a, b, dims, preferred_element_type=F32)


def attend_rows(q_ref, g_ref, k_lo, k_hi, v_lo, v_hi, doc_ref, first, o_ref, dq_ref, lse_ref, dk_ref, dv_ref, p_s, ds_s):
    heads = q_ref.shape[1] // HEAD
    scale = HEAD ** (-0.5)
    keys = jnp.concatenate([k_lo[...], k_hi[...]], axis=0)
    vals = jnp.concatenate([v_lo[...], v_hi[...]], axis=0)
    docs = [doc_ref[pl.ds(jnp.maximum(first + b, 0), 1), :].astype(F32) for b in range((2 * REACH) // BLOCK)]
    docs = [jnp.broadcast_to(jnp.where(first + b >= 0, d, -1.0), (BLOCK, BLOCK)) for b, d in enumerate(docs)]
    docs_t = [d.T for d in docs]
    keys_t = keys.T
    vals_t = vals.T
    dk_ref[...] = jnp.zeros_like(dk_ref)
    dv_ref[...] = jnp.zeros_like(dv_ref)
    for j in range(REACH // BLOCK):
        lo = j * BLOCK
        rows = slice(lo, lo + BLOCK)
        win = slice(lo, lo + WINDOW)
        k_w, v_w = keys[win], vals[win]
        kt_w, vt_w = keys_t[:, win], vals_t[:, win]
        key_at = lax.broadcasted_iota(jnp.int32, (WINDOW, BLOCK), 0)
        query_at = lax.broadcasted_iota(jnp.int32, (WINDOW, BLOCK), 1) + REACH
        own = docs[j + REACH // BLOCK]
        same = jnp.concatenate([jnp.where(d == own, 1.0, 0.0) for d in docs_t[j : j + WINDOW // BLOCK]], axis=0)
        allowed = (same > 0.5) & (key_at <= query_at)
        bias = jnp.where(allowed, 0.0, -1e30).astype(F32)
        bias = jnp.concatenate([bias, bias], axis=1)
        q_parts, g_parts = [], []
        for h in range(0, heads, 2):
            c0 = slice(h * HEAD, (h + 1) * HEAD)
            c1 = slice((h + 1) * HEAD, (h + 2) * HEAD)
            qp = jnp.concatenate([q_ref[rows, c0], q_ref[rows, c1]], axis=0)
            gp = jnp.concatenate([g_ref[rows, c0], g_ref[rows, c1]], axis=0)
            q_parts.append(qp)
            g_parts.append(gp)
            s = dot(k_w, qp, NT) * scale + bias
            top = jnp.max(s, axis=0, keepdims=True)
            e = jnp.exp(s - top)
            total = jnp.sum(e, axis=0, keepdims=True)
            lse = top + jnp.log(total)
            lse_ref[h : h + 1, rows] = lse[:, :BLOCK]
            lse_ref[h + 1 : h + 2, rows] = lse[:, BLOCK:]
            p = e * (1.0 / total)
            dp = dot(v_w, gp, NT)
            delta = jnp.sum(p * dp, axis=0, keepdims=True)
            ds = (p * (dp - delta)).astype(BF16)
            p_low = p.astype(BF16)
            cols = slice(h * BLOCK, (h + 2) * BLOCK)
            p_s[:, cols] = p_low
            ds_s[:, cols] = ds
            o = dot(vt_w, p_low).T
            o_ref[rows, c0] = o[:BLOCK].astype(BF16)
            o_ref[rows, c1] = o[BLOCK:].astype(BF16)
            dq = (dot(kt_w, ds) * scale).T
            dq_ref[rows, c0] = dq[:BLOCK].astype(BF16)
            dq_ref[rows, c1] = dq[BLOCK:].astype(BF16)
        dv_ref[win, :] += dot(p_s[...], jnp.concatenate(g_parts, axis=0))
        dk_ref[win, :] += dot(ds_s[...], jnp.concatenate(q_parts, axis=0)) * scale


def early_kernel(q, g, k_lo, k_hi, v_lo, v_hi, doc, o, dq, lse, dk_own, dv_own, back, p_s, ds_s, dk, dv):
    first = lax.axis_index("dp") * (2 * REACH // BLOCK) - REACH // BLOCK
    attend_rows(q, g, k_lo, k_hi, v_lo, v_hi, doc, first, o, dq, lse, dk, dv, p_s, ds_s)
    back[:, :HEAD] = dk[:REACH].astype(BF16)
    back[:, HEAD:] = dv[:REACH].astype(BF16)
    dk_own[...] = dk[REACH:]
    dv_own[...] = dv[REACH:]


def late_kernel(q, g, k_lo, k_hi, v_lo, v_hi, doc, dk_own, dv_own, o_in, dq_in, lse_in, o, dq, lse, low, high, p_s, ds_s, dk, dv):
    first = lax.axis_index("dp") * (2 * REACH // BLOCK)
    attend_rows(q, g, k_lo, k_hi, v_lo, v_hi, doc, first, o, dq, lse, dk, dv, p_s, ds_s)
    low[:, :HEAD] = (dk[:REACH] + dk_own[...]).astype(BF16)
    low[:, HEAD:] = (dv[:REACH] + dv_own[...]).astype(BF16)
    high[:, :HEAD] = dk[REACH:]
    high[:, HEAD:] = dv[REACH:]


def spec(shape, at):
    return pl.BlockSpec(shape, lambda i: at)


def attention(queries, out_grad, key_rows, value_matrix, prior, docs):
    tok, width = queries.shape
    heads = width // HEAD
    half = tok // 2
    cost = pl.CostEstimate(flops=6 * 2 * half * WINDOW * width, bytes_accessed=32 << 20, transcendentals=half * WINDOW * heads)
    params = pltpu.CompilerParams(vmem_limit_bytes=60 << 20)
    wide = lambda i: spec((half, width), (i, 0))
    kv = lambda i: spec((half, HEAD), (i, 0))
    doc = spec(docs.shape, (0, 0))
    scratch = [pltpu.VMEM((WINDOW, heads * BLOCK), BF16)] * 2 + [pltpu.VMEM((tok, HEAD), F32)] * 2
    rows_out = jax.ShapeDtypeStruct((tok, width), BF16)
    lse_out = jax.ShapeDtypeStruct((heads, tok), F32)
    grad = jax.ShapeDtypeStruct((half, HEAD), F32)
    part = spec((half, HEAD), (0, 0))
    pair = spec((half, 2 * HEAD), (0, 0))
    o, dq, lse, dk_own, dv_own, back = pl.pallas_call(
        early_kernel,
        grid=(1,),
        in_specs=[wide(0), wide(0), kv(0), kv(0), spec((half, HEAD), (0, 1)), kv(0), doc],
        out_specs=[wide(0), wide(0), spec((heads, half), (0, 0)), part, part, pair],
        out_shape=[rows_out, rows_out, lse_out, grad, grad, jax.ShapeDtypeStruct((half, 2 * HEAD), BF16)],
        scratch_shapes=scratch,
        cost_estimate=cost,
        compiler_params=params,
        name="attend_early",
    )(queries, out_grad, prior, key_rows, prior, value_matrix, docs)
    hbm = pl.BlockSpec(memory_space=pl.ANY)
    o, dq, lse, low, high = pl.pallas_call(
        late_kernel,
        grid=(1,),
        in_specs=[wide(1), wide(1), kv(0), kv(1), kv(0), kv(1), doc, part, part, hbm, hbm, hbm],
        out_specs=[wide(1), wide(1), spec((heads, half), (0, 1)), pair, pair],
        out_shape=[rows_out, rows_out, lse_out, jax.ShapeDtypeStruct((half, 2 * HEAD), BF16), jax.ShapeDtypeStruct((half, 2 * HEAD), F32)],
        scratch_shapes=scratch,
        input_output_aliases={9: 0, 10: 1, 11: 2},
        cost_estimate=cost,
        compiler_params=params,
        name="attend_late",
    )(queries, out_grad, key_rows, key_rows, value_matrix, value_matrix, docs, dk_own, dv_own, o, dq, lse)
    return o, dq, lse, back, low, high, dk_own


def tail_kernel(k, v, out):
    out[:, :HEAD] = k[...]
    out[:, HEAD:] = v[...]


def pack_tail(key_rows, value_matrix):
    half = key_rows.shape[0] // 2
    return pl.pallas_call(
        tail_kernel,
        grid=(1,),
        in_specs=[spec((half, HEAD), (1, 0))] * 2,
        out_specs=spec((half, 2 * HEAD), (0, 0)),
        out_shape=jax.ShapeDtypeStruct((half, 2 * HEAD), BF16),
        name="pack_tail",
    )(key_rows, value_matrix)


def split_kernel(x, first, second):
    half = first.shape[0]
    first[...] = x[:, :half].T
    second[...] = x[:, half:].T


def split_inputs(inputs):
    tok, width = inputs.shape
    shape = (width // 2, tok)
    part = jax.ShapeDtypeStruct(shape, BF16)
    return pl.pallas_call(
        split_kernel,
        grid=(1,),
        in_specs=[spec((tok, width), (0, 0))],
        out_specs=[spec(shape, (0, 0))] * 2,
        out_shape=[part, part],
        compiler_params=pltpu.CompilerParams(vmem_limit_bytes=48 << 20),
        name="split_inputs",
    )(inputs)


def join_kernel(low, high, back, joined, key_grad, value_grad):
    half = low.shape[0]
    rest = (high[...] + back[...].astype(F32)).astype(BF16)
    joined[:half] = low[...]
    joined[half:] = rest
    key_grad[:half] = low[:, :HEAD]
    key_grad[half:] = rest[:, :HEAD]
    value_grad[:half] = low[:, HEAD:]
    value_grad[half:] = rest[:, HEAD:]


def join_gradients(low, high, back):
    half, width = low.shape
    part = spec((half, width), (0, 0))
    shapes = [(2 * half, width), (2 * half, HEAD), (2 * half, HEAD)]
    return pl.pallas_call(
        join_kernel,
        grid=(1,),
        in_specs=[part] * 3,
        out_specs=[spec(shape, (0, 0)) for shape in shapes],
        out_shape=[jax.ShapeDtypeStruct(shape, BF16) for shape in shapes],
        name="join_gradients",
    )(low, high, back)


def weight_kernel(a0, a1, a3, a2, d0, d1, d3, d2, b0, b1, b3, b2, c0, c1, c3, c2, out):
    core = lax.rem(lax.axis_index("tensor"), 2)
    mine = pl.ds(pl.multiple_of(core * 2 * HEAD, 2 * HEAD), 2 * HEAD)
    other = pl.ds(pl.multiple_of((1 - core) * 2 * HEAD, 2 * HEAD), 2 * HEAD)

    def multiply(left):
        right = [jnp.concatenate([b[...], c[...]], axis=1) for b, c in zip((b0, b1, b3, b2), (c0, c1, c3, c2))]
        total = dot(jnp.concatenate([l[...] for l in left], axis=1), jnp.concatenate(right, axis=0))
        out[:, mine] = total[:, : 2 * HEAD].astype(BF16)
        out[:, other] = total[:, 2 * HEAD :].astype(BF16)

    steps = pl.num_programs(0) // 2

    @pl.when(pl.program_id(0) < steps)
    def _():
        multiply((a0, a1, a3, a2))

    @pl.when(pl.program_id(0) >= steps)
    def _():
        multiply((d0, d1, d3, d2))


def weight_partial(first, second, mine, other):
    tile = 4 * HEAD
    width, tok = first[0].shape
    steps = width // tile
    low = pl.BlockSpec((tile, tok), lambda i: (jnp.minimum(i, steps - 1), 0))
    high = pl.BlockSpec((tile, tok), lambda i: (jnp.maximum(i - steps, 0), 0))
    whole = pl.BlockSpec((tok, 2 * HEAD), lambda i: (0, 0))
    return pl.pallas_call(
        weight_kernel,
        grid=(2 * steps,),
        in_specs=[low] * 4 + [high] * 4 + [whole] * 8,
        out_specs=pl.BlockSpec((tile, 4 * HEAD), lambda i: (i, 0)),
        out_shape=jax.ShapeDtypeStruct((2 * width, 4 * HEAD), BF16),
        cost_estimate=pl.CostEstimate(flops=4 * width * 4 * HEAD * 4 * tok, bytes_accessed=8 << 20, transcendentals=0),
        compiler_params=pltpu.CompilerParams(vmem_limit_bytes=60 << 20),
        name="weight_partial",
    )(*first, *second, *mine, *other)


def sum_kernel(parts, out):
    y = lax.axis_index("tensor") // 2
    wide = 2 * HEAD
    for head in range(2 * NX):
        x = lax.rem(head // 2 - y + NX + 2 * (head % 2), NX)
        side = slice((head % 2) * wide, (head % 2 + 1) * wide)
        total = parts[x, :, side].astype(F32)
        for z in range(1, NZ):
            total += parts[z * NX + x, :, side].astype(F32)
        out[:, head * wide : (head + 1) * wide] = total


def sum_parts(parts):
    sources, rows, width = parts.shape
    return pl.pallas_call(
        sum_kernel,
        grid=(1,),
        in_specs=[spec((sources, rows, width), (0, 0, 0))],
        out_specs=spec((rows, NX * width), (0, 0)),
        out_shape=jax.ShapeDtypeStruct((rows, NX * width), F32),
        cost_estimate=pl.CostEstimate(flops=sources * rows * width, bytes_accessed=2 << 20, transcendentals=0),
        compiler_params=pltpu.CompilerParams(vmem_limit_bytes=60 << 20),
        name="sum_parts",
    )(parts)


def along_x(steps):
    return [(z * NX + x, z * NX + (x + steps) % NX) for z in range(NZ) for x in range(NX)]


def to_columns(steps):
    pairs = []
    for z in range(NZ):
        for x in range(NX):
            for y in range(NY):
                for c in range(2):
                    x_to = (x + steps) % NX
                    y_to = (y - x_to - 2 * c) % NY
                    pairs.append((((z * NX + x) * NY + y) * 2 + c, ((z * NX + x_to) * NY + y_to) * 2 + c))
    return pairs


def after(value, *others):
    return lax.optimization_barrier((value, *others))[0]


def body(queries, key_rows, value_matrix, out_grad, inputs, doc_ids):
    shards = lax.axis_size("dp")
    docs = doc_ids.reshape(-1, BLOCK)
    onward = [(i, i + 1) for i in range(shards - 1)]
    backward = [(i + 1, i) for i in range(shards - 1)]
    prior = lax.ppermute(pack_tail(key_rows, value_matrix), "dp", onward)

    first, second = split_inputs(inputs)
    first_sent = after(first, prior)
    first_left = lax.ppermute(first_sent, "dp", along_x(1))
    first_right = lax.ppermute(first_sent, "dp", along_x(-1))

    out_rows, query_grad, logsum, back, low, high, dk_early = attention(
        queries, out_grad, key_rows, value_matrix, prior, docs
    )
    second_left = lax.ppermute(after(second, dk_early), "dp", along_x(1))
    back = lax.ppermute(back, "dp", backward)
    second_right = lax.ppermute(after(second, back), "dp", along_x(-1))
    first_far = lax.ppermute(after(first_left, low), "dp", along_x(1))
    second_far = lax.ppermute(second_right, "dp", along_x(-1))
    joined, key_gradient, value_gradient = join_gradients(low, high, after(back, first_right))

    mine = [lax.ppermute(joined, ("dp", "tensor"), to_columns(d)) for d in ORDER]
    swap = [(t, t ^ 1) for t in range(2 * NY)]
    other = [lax.ppermute(m, "tensor", swap) for m in mine]
    first_all = (first, first_left, first_right, first_far)
    second_all = (second, second_left, second_right, second_far)
    partial = weight_partial(first_all, second_all, mine, other)
    parts = lax.all_to_all(partial, "dp", 0, 0, tiled=True)
    weight_grad = sum_parts(parts.reshape(shards, -1, 4 * HEAD))
    return out_rows, query_grad, key_gradient, value_gradient, logsum, weight_grad


def solution(mesh):
    split = P("dp", "tensor")
    return jax.shard_map(
        body,
        mesh=mesh,
        in_specs=(split, split, split, split, split, P()),
        out_specs=(split, split, split, split, P("tensor", "dp"), P(("tensor", "dp"), None)),
        check_vma=False,
    )
```
